32 devices in a mesh: wide: 16 (over z, y, x), narrow: 2 (over core).
Axes of the slice: x: 2, y: 2, z: 4, core: 2. Of those that a mesh axis runs over, the one named last changes fastest.
Arguments:
- voltages: bfloat16 [512, 1048576], P('wide', 'narrow'), may hold values from -6 to 6
- following: bfloat16 [512, 30720], P('wide'), may hold values from -6 to 6
Outputs:
- visibilities: float32 [1024, 2, 512, 512], P(('wide', 'narrow'))
The draws below stay inside these ranges and needn't reach their ends.
All inputs are finite; a program needn't handle non-finite values.
Results may differ from the reference program's by a relative error of at most 0.0028.
Values may be sent and summed in bfloat16 or wider, within the bound.
No kernel may reach another device: no remote copies, remote signals or barrier semaphores. Data moves between devices by JAX's collectives and lax.ppermute only.
A program may use at most 384 MiB of HBM per device.

```python
import math
import jax
import jax.numpy as jnp
from jax import lax

FFT_LEN = 2048
CHANNELS = 1024
TAPS = 16
INPUTS = 512
SPECTRA = 512
SAMPLES = 1048576


def shard_levels(stream_key, dims, shards, smallest, high):
    loudness = 1.0
    for axis_at, blocks in shards:
        steps = jax.random.uniform(jax.random.fold_in(jax.random.fold_in(stream_key, 6), axis_at), (blocks,), jnp.float32, smallest / len(shards), high / len(shards))
        loudness = loudness * jnp.repeat(jnp.exp(steps), dims[axis_at] // blocks).reshape((-1,) + (1,) * (len(dims) - 1 - axis_at))
    return loudness


def bell_draw(key, extent, scale, bound, shards=(), held_as=jnp.bfloat16):
    array = jax.random.normal(key, extent, jnp.float32) * scale
    if len(shards) > 0:
        array = shard_levels(key, extent, shards, -0.22, 0.18) * array
    return jnp.clip(array, min=-bound, max=bound).astype(held_as)


def setup_inputs(seed: int = 0) -> dict:
    key_list = jax.random.split(jax.random.key(seed), 3)
    return {
        "voltages": bell_draw(key_list[0], (INPUTS, SAMPLES), 1.0, 6.0, ((0, 16), (1, 2))),
        "following": bell_draw(key_list[1], (INPUTS, (TAPS - 1) * FFT_LEN), 1.0, 6.0, ((0, 16),)),
    }


def pfb_window(block_len, tap_count):
    length_all = tap_count * block_len
    sample_pos = jnp.arange(length_all, dtype=jnp.float32)
    centred = (sample_pos + 0.5 - length_all / 2.0) / block_len
    taper = 0.5 - 0.5 * jnp.cos(2.0 * jnp.pi * (sample_pos + 0.5) / length_all)
    return jnp.sinc(centred) * taper

def reference(voltages, following):
    weights_taps = pfb_window(FFT_LEN, TAPS).reshape(TAPS, FFT_LEN)
    extended = jnp.concatenate([voltages, following], axis=1)
    scaling = 1.0 / math.sqrt(FFT_LEN)

    def one_input(series):
        blocks = series.astype(jnp.float32).reshape(SPECTRA + TAPS - 1, FFT_LEN)
        filtered = jnp.zeros((SPECTRA, FFT_LEN), jnp.float32)
        for tap_index in range(TAPS):
            filtered = filtered + weights_taps[tap_index][None, :] * blocks[tap_index:tap_index + SPECTRA]
        spectrum = jnp.fft.rfft(filtered, axis=-1)[:, :CHANNELS] * scaling
        return (jnp.real(spectrum).astype(jnp.bfloat16), jnp.imag(spectrum).astype(jnp.bfloat16))
    real_part, imag_part = lax.map(one_input, extended)
    half = INPUTS

    def channel_block(first):
        real_block = lax.dynamic_slice_in_dim(real_part, first, 8, 2)
        imag_block = lax.dynamic_slice_in_dim(imag_part, first, 8, 2)
        stacked = jnp.concatenate([real_block, imag_block], axis=0).astype(jnp.float32)
        gram = jnp.einsum('isc,jsc->cij', stacked, stacked, precision=lax.Precision.HIGHEST)
        vis_real = gram[:, :half, :half] + gram[:, half:, half:]
        vis_imag = gram[:, half:, :half] - gram[:, :half, half:]
        return jnp.stack([vis_real, vis_imag], axis=1) / SPECTRA
    starts = (jnp.arange(CHANNELS // 8) * 8).astype(jnp.int32)
    result = lax.map(channel_block, starts)
    return result.reshape(CHANNELS, 2, INPUTS, INPUTS)
```

```python
import functools
import math

import jax
import jax.numpy as jnp
import ml_dtypes
import numpy as np
from jax import lax
from jax.experimental import pallas as pl
from jax.experimental.pallas import tpu as pltpu
from jax.sharding import PartitionSpec as P

FFT_LEN = 2048
CHANNELS = 1024
TAPS = 16
FOLD = FFT_LEN // 2
SPAN = 128
GROUPS = 4
BATCH = 8
COLS = 256
VMEM = 56 * 1024 * 1024
AXES = ("wide", "narrow")


def pfb_window():
    n = np.arange(TAPS * FFT_LEN, dtype=np.float64)
    total = TAPS * FFT_LEN
    taper = 0.5 - 0.5 * np.cos(2.0 * np.pi * (n + 0.5) / total)
    window = np.sinc((n + 0.5 - total / 2) / FFT_LEN) * taper
    return window.astype(np.float32).reshape(TAPS, FFT_LEN)


def split16(values):
    high = values.astype(ml_dtypes.bfloat16)
    low = (values - high.astype(np.float64)).astype(ml_dtypes.bfloat16)
    return high, low


def dft_tables(n_dev):
    chan_dev = CHANNELS // n_dev
    cg = chan_dev // GROUPS
    g, p, d, h = np.meshgrid(
        np.arange(GROUPS), np.arange(2), np.arange(n_dev), np.arange(cg // 2), indexing="ij"
    )
    chan = d * chan_dev + g * cg + 2 * h + p
    turns = chan[..., None] * np.arange(FOLD) % FFT_LEN
    angles = 2.0 * np.pi * turns / FFT_LEN
    table = np.stack([np.cos(angles), -np.sin(angles)], axis=-2) / math.sqrt(FFT_LEN)
    return split16(table.reshape(GROUPS, 2, CHANNELS // GROUPS, FOLD))


def filter_kernel(x_ref, halo_ref, w_ref, *rest):
    f_ref, even_ref, odd_ref = rest[-3:]
    n_in = x_ref.shape[0]
    column0 = pl.program_id(0) * COLS

    def load(ref, t, k):
        tile = ref[:, pl.ds(pl.multiple_of(t * FFT_LEN + k, 128), 128)].astype(jnp.float32)
        return tile.reshape(n_in // 8, 8, 128)

    def fir(tiles, k):
        weights = [w_ref[p, :, pl.ds(pl.multiple_of(k, 128), 128)][None] for p in range(TAPS)]
        outs = []
        for j in range(BATCH):
            total = weights[0] * tiles[j]
            for p in range(1, TAPS):
                total = total + weights[p] * tiles[j + p]
            outs.append(total)
        return outs

    def emit(m0, first, second):
        for j in range(BATCH):
            rows = pl.ds(m0 + j, n_in, stride=SPAN)
            even_ref[rows, :] = (first[j] + second[j]).reshape(n_in, 128)
            odd_ref[rows, :] = (first[j] - second[j]).reshape(n_in, 128)

    inner = (SPAN - TAPS + 1) // BATCH
    for kt in range(COLS // 128):
        k = column0 + kt * 128

        def body(step, _, k=k):
            m0 = step * BATCH
            both = []
            for kk in (k, k + FOLD):
                both.append(fir([load(x_ref, m0 + t, kk) for t in range(BATCH + TAPS - 1)], kk))
            emit(m0, *both)
            return 0

        lax.fori_loop(0, inner, body, 0)
        for step in range(inner, SPAN // BATCH):
            m0 = step * BATCH
            both = []
            for kk in (k, k + FOLD):
                tiles = []
                for t in range(m0, m0 + BATCH + TAPS - 1):
                    tiles.append(load(x_ref, t, kk) if t < SPAN else load(halo_ref, t - SPAN, kk))
                both.append(fir(tiles, kk))
            emit(m0, *both)

        def split(step, _, kt=kt):
            rows = pl.ds(pl.multiple_of(step * 256, 256), 256)
            for p, ref in ((0, even_ref), (1, odd_ref)):
                value = ref[rows, :]
                high = value.astype(jnp.bfloat16)
                low = (value - high.astype(jnp.float32)).astype(jnp.bfloat16)
                f_ref[p, 0, rows, pl.ds(kt * 128, 128)] = high
                f_ref[p, 1, rows, pl.ds(kt * 128, 128)] = low
            return 0

        lax.fori_loop(0, n_in * SPAN // 256, split, 0)


def filter_unit(voltages, after, weights, n_in, ig, half, halves, deps):
    width = SPAN * FFT_LEN
    if half == halves - 1:
        halo = after
        halo_spec = pl.BlockSpec((n_in, after.shape[1]), lambda i: (ig, 0))
    else:
        halo = voltages
        halo_spec = pl.BlockSpec((n_in, TAPS * FFT_LEN), lambda i: (ig, (half + 1) * SPAN // TAPS))
    rows = n_in * SPAN
    return pl.pallas_call(
        filter_kernel,
        grid=(FOLD // COLS,),
        in_specs=[
            pl.BlockSpec((n_in, width), lambda i: (ig, half)),
            halo_spec,
            pl.BlockSpec((TAPS, 8, FFT_LEN), lambda i: (0, 0, 0)),
        ]
        + [pl.BlockSpec(memory_space=pl.ANY)] * len(deps),
        out_specs=pl.BlockSpec((2, 2, rows, COLS), lambda i: (0, 0, 0, i)),
        out_shape=jax.ShapeDtypeStruct((2, 2, rows, FOLD), jnp.bfloat16),
        scratch_shapes=[pltpu.VMEM((rows, 128), jnp.float32)] * 2,
        compiler_params=pltpu.CompilerParams(vmem_limit_bytes=VMEM),
        cost_estimate=pl.CostEstimate(
            flops=rows * FFT_LEN * TAPS * 2, bytes_accessed=rows * FFT_LEN * 6, transcendentals=0
        ),
        name="filter",
    )(voltages, halo, weights, *deps)


def dft_kernel(f_ref, high_ref, low_ref, *rest):
    out_ref, held_ref = rest[-2:]
    step = pl.program_id(2)
    n_in = out_ref.shape[-2]
    n_rows = high_ref.shape[2]
    n_here = f_ref.shape[2] // SPAN
    dims = (((1,), (1,)), ((), ()))
    for pair in range(0, n_here, 2):
        take = min(2, n_here - pair)
        rows = pl.ds(pair * SPAN, take * SPAN)
        f_high = f_ref[0, 0, rows, :]
        f_low = f_ref[0, 1, rows, :]
        total = lax.dot_general(high_ref[0, 0], f_high, dims, preferred_element_type=jnp.float32)
        total += lax.dot_general(high_ref[0, 0], f_low, dims, preferred_element_type=jnp.float32)
        total += lax.dot_general(low_ref[0, 0], f_high, dims, preferred_element_type=jnp.float32)
        for j in range(take):
            at = step * n_here + pair + j
            held_ref[pl.ds(at, n_rows, stride=n_in), :] = total[:, j * SPAN : (j + 1) * SPAN]

    @pl.when(step == pl.num_programs(2) - 1)
    def _():
        n_dev, _, _, n_pair, _, _, _ = out_ref.shape
        for d in range(n_dev):
            each = n_pair * 2 * n_in
            block = held_ref[pl.ds(d * each, each), :].astype(jnp.bfloat16)
            out_ref[d, 0, 0] = block.reshape(n_pair, 2, n_in, SPAN)


def dft_unit(folded, tables, n_dev, n_in, g0, n_groups, deps):
    chan_dev = CHANNELS // n_dev
    n_pair = chan_dev // GROUPS // 2
    n_rows = CHANNELS // GROUPS
    here = min(4, n_in)
    f_rows = here * SPAN
    table_spec = pl.BlockSpec((1, 1, n_rows, FOLD), lambda g, p, i: (g0 + g, p, 0, 0))
    return pl.pallas_call(
        dft_kernel,
        grid=(n_groups, 2, n_in // here),
        in_specs=[
            pl.BlockSpec((1, 2, f_rows, FOLD), lambda g, p, i: (p, 0, i, 0)),
            table_spec,
            table_spec,
        ]
        + [pl.BlockSpec(memory_space=pl.ANY)] * len(deps),
        out_specs=pl.BlockSpec(
            (n_dev, 1, 1, n_pair, 2, n_in, SPAN), lambda g, p, i: (0, g, p, 0, 0, 0, 0)
        ),
        out_shape=jax.ShapeDtypeStruct(
            (n_dev, n_groups, 2, n_pair, 2, n_in, SPAN), jnp.bfloat16
        ),
        scratch_shapes=[pltpu.VMEM((n_rows * n_in, SPAN), jnp.float32)],
        compiler_params=pltpu.CompilerParams(vmem_limit_bytes=VMEM),
        cost_estimate=pl.CostEstimate(
            flops=n_groups * 12 * n_rows * n_in * SPAN * FOLD,
            bytes_accessed=n_groups * n_in * SPAN * FOLD * 8,
            transcendentals=0,
        ),
        name="dft",
    )(folded, *tables, *deps)


def gram_kernel(n_units, halves, n_wide, n_narrow, n_in, time_len, *refs):
    units = refs[:n_units]
    out_ref, left_ref, right_ref = refs[-3:]
    local_inputs = n_in * (n_units // halves)
    for w in range(n_wide):
        for n in range(n_narrow):
            for u in range(n_units):
                ig, half = u // halves, u % halves
                row = pl.ds(w * local_inputs + ig * n_in, n_in)
                at = (n * halves + half) * SPAN
                real = units[u][w * n_narrow + n, 0, 0, 0, 0]
                imag = units[u][w * n_narrow + n, 0, 0, 0, 1]
                right_ref[row, pl.ds(at, SPAN)] = real
                right_ref[row, pl.ds(time_len + at, SPAN)] = imag
                left_ref[row, pl.ds(at, SPAN)] = imag
                left_ref[row, pl.ds(time_len + at, SPAN)] = -real
    dims = (((1,), (1,)), ((), ()))
    right = right_ref[...]
    scale = 1.0 / time_len
    out_ref[0, 0] = lax.dot_general(right, right, dims, preferred_element_type=jnp.float32) * scale
    out_ref[0, 1] = (
        lax.dot_general(left_ref[...], right, dims, preferred_element_type=jnp.float32) * scale
    )


def gram_group(units, places, previous, n_wide, n_narrow, halves, group, n_in):
    n_dev = n_wide * n_narrow
    chan_dev = CHANNELS // n_dev
    cg = chan_dev // GROUPS
    n_units = len(units)
    inputs = n_wide * n_in * (n_units // halves)
    time_len = n_narrow * halves * SPAN
    specs = [
        pl.BlockSpec(
            (n_dev, 1, 1, 1, 2, n_in, SPAN), lambda t, at=at: (0, at, t % 2, t // 2, 0, 0, 0)
        )
        for at in places
    ]
    args = list(units)
    aliases = {}
    if previous is not None:
        specs.append(pl.BlockSpec(memory_space=pl.ANY))
        args.append(previous)
        aliases = {n_units: 0}
    return pl.pallas_call(
        functools.partial(gram_kernel, n_units, halves, n_wide, n_narrow, n_in, time_len),
        grid=(cg,),
        in_specs=specs,
        out_specs=pl.BlockSpec((1, 2, inputs, inputs), lambda t: (group * cg + t, 0, 0, 0)),
        out_shape=jax.ShapeDtypeStruct((chan_dev, 2, inputs, inputs), jnp.float32),
        scratch_shapes=[pltpu.VMEM((inputs, 2 * time_len), jnp.bfloat16)] * 2,
        input_output_aliases=aliases,
        compiler_params=pltpu.CompilerParams(vmem_limit_bytes=VMEM),
        cost_estimate=pl.CostEstimate(
            flops=cg * 8 * inputs * inputs * time_len,
            bytes_accessed=cg * inputs * (8 * inputs + 4 * time_len),
            transcendentals=0,
        ),
        name="gram",
    )(*args)


def shards(voltages, following):
    n_wide, n_narrow = lax.axis_size("wide"), lax.axis_size("narrow")
    n_dev = n_wide * n_narrow
    local_inputs, local_span = voltages.shape
    halves = local_span // (SPAN * FFT_LEN)
    n_in = min(16, local_inputs)
    in_groups = local_inputs // n_in

    leading = voltages[:, : (TAPS - 1) * FFT_LEN]
    shifted = lax.ppermute(leading, "narrow", [(i, i - 1) for i in range(1, n_narrow)])
    is_final = lax.axis_index("narrow") == n_narrow - 1
    after = jnp.where(is_final, following, shifted)

    tables = [jnp.asarray(t) for t in dft_tables(n_dev)]
    weights = jnp.asarray(np.broadcast_to(pfb_window()[:, None, :], (TAPS, 8, FFT_LEN)))

    order = [(ig, half) for half in range(halves) for ig in range(in_groups)]
    parts = []
    for index in range(len(order)):
        count = GROUPS if index in (0, len(order) - 1) else 1
        size = GROUPS // count
        parts += [(index, first, size) for first in range(0, GROUPS, size)]

    received = []
    folded = {}
    for job, (index, first, size) in enumerate(parts):
        if index not in folded:
            ig, half = order[index]
            deps = [received[job - 3]] if job >= 3 else []
            folded[index] = filter_unit(voltages, after, weights, n_in, ig, half, halves, deps)
        deps = [received[job - 2]] if job >= 2 else []
        spectra = dft_unit(folded[index], tables, n_dev, n_in, first, size, deps)
        received.append(lax.all_to_all(spectra, AXES, split_axis=0, concat_axis=0, tiled=True))

    result = None
    for group in range(GROUPS):
        units, places = [], []
        for ig in range(in_groups):
            for half in range(halves):
                index = order.index((ig, half))
                for job, (at, first, size) in enumerate(parts):
                    if at == index and first <= group < first + size:
                        units.append(received[job])
                        places.append(group - first)
        result = gram_group(
            units, places, result, n_wide, n_narrow, halves, group, n_in
        )
    return result


def solution(mesh):
    in_specs = (P("wide", "narrow"), P("wide", None))
    out_specs = P(("wide", "narrow"), None, None, None)
    return jax.shard_map(shards, mesh=mesh, in_specs=in_specs, out_specs=out_specs, check_vma=False)
```

```python
import functools
import math

import jax
import jax.numpy as jnp
import ml_dtypes
import numpy as np
from jax import lax
from jax.experimental import pallas as pl
from jax.experimental.pallas import tpu as pltpu
from jax.sharding import PartitionSpec as P

FFT_LEN = 2048
CHANNELS = 1024
TAPS = 16
FOLD = FFT_LEN // 2
SPAN = 128
GROUPS = 4
BATCH = 8
STRETCH = 32
COLS = 256
VMEM = 127 * 512 * 1024
AXES = ("wide", "narrow")


def odd_stride(rows):
    return rows + 8 * (1 - rows // 8 % 2)


def pfb_window():
    n = np.arange(TAPS * FFT_LEN, dtype=np.float64)
    total = TAPS * FFT_LEN
    taper = 0.5 - 0.5 * np.cos(2.0 * np.pi * (n + 0.5) / total)
    window = np.sinc((n + 0.5 - total / 2) / FFT_LEN) * taper
    return window.astype(np.float32).reshape(TAPS, FFT_LEN)


def split16(values):
    high = values.astype(ml_dtypes.bfloat16)
    low = (values - high.astype(np.float64)).astype(ml_dtypes.bfloat16)
    return high, low


def dft_table(n_dev):
    chan_dev = CHANNELS // n_dev
    cg = chan_dev // GROUPS
    g, p, d, h = np.meshgrid(
        np.arange(GROUPS), np.arange(2), np.arange(n_dev), np.arange(cg // 2), indexing="ij"
    )
    chan = d * chan_dev + g * cg + 2 * h + p
    turns = chan[..., None] * np.arange(FOLD) % FFT_LEN
    angles = 2.0 * np.pi * turns / FFT_LEN
    table = np.stack([np.cos(angles), -np.sin(angles)], axis=-2) / math.sqrt(FFT_LEN)
    return np.concatenate(split16(table.reshape(GROUPS, 2, CHANNELS // GROUPS, FOLD)), axis=2)


def filter_kernel(first, n_in, with_after, x_ref, w_ref, halo_ref, *rest):
    outs, (even_ref, odd_ref, tail_ref) = rest[-7:-3], rest[-3:]
    n_rows = x_ref.shape[0]
    pitch = odd_stride(STRETCH)
    halo_len = (TAPS - 1) * FFT_LEN
    if with_after:
        is_last = pl.program_id(0) == pl.num_programs(0) - 1

        @pl.when(is_last)
        def _():
            tail_ref[...] = rest[0][:, :halo_len]

        @pl.when(jnp.logical_not(is_last))
        def _():
            tail_ref[...] = halo_ref[:, :halo_len]

        next_ref = tail_ref
    else:
        next_ref = halo_ref

    def load(t, k):
        ref, at = (x_ref, t) if t < STRETCH else (next_ref, t - STRETCH)
        tile = ref[:, pl.ds(pl.multiple_of(at * FFT_LEN + k, 128), 128)].astype(jnp.float32)
        return tile.reshape(n_rows // 8, 8, 128)[first // 8 : (first + n_in) // 8]

    def fir(m0, k):
        weights = [w_ref[p, :, pl.ds(pl.multiple_of(k, 128), 128)][None] for p in range(TAPS)]
        sums = [None] * BATCH
        for t in range(BATCH + TAPS - 1):
            tile = load(m0 + t, k)
            for j in range(max(0, t - TAPS + 1), min(BATCH, t + 1)):
                term = weights[t - j] * tile
                sums[j] = term if sums[j] is None else sums[j] + term
        return sums

    def columns(kt, _):
        k = kt * 128
        for m0 in range(0, STRETCH, BATCH):
            lower, upper = fir(m0, k), fir(m0, k + FOLD)
            for j in range(BATCH):
                rows = pl.ds(m0 + j, n_in, stride=pitch)
                even_ref[rows, :] = (lower[j] + upper[j]).reshape(n_in, 128)
                odd_ref[rows, :] = (lower[j] - upper[j]).reshape(n_in, 128)
        chunk, at = kt // (COLS // 128), pl.ds(pl.multiple_of(kt % (COLS // 128) * 128, 128), 128)
        for i in range(n_in):
            for p, ref in ((0, even_ref), (1, odd_ref)):
                value = ref[pl.ds(i * pitch, STRETCH), :]
                high = value.astype(jnp.bfloat16)
                low = (value - high.astype(jnp.float32)).astype(jnp.bfloat16)
                outs[2 * p][chunk, i, :, at] = high
                outs[2 * p + 1][chunk, i, :, at] = low
        return 0

    lax.fori_loop(0, FOLD // 128, columns, 0)


def filter_unit(voltages, after, weights, start, n_in, half, halves, deps):
    n_block = min(16, voltages.shape[0])
    ig = start // n_block
    steps = SPAN // STRETCH
    scale = STRETCH // TAPS
    last_halo = voltages.shape[1] // (TAPS * FFT_LEN) - 1
    with_after = half == halves - 1

    def halo_at(t):
        return (ig, jnp.minimum((half * steps + t + 1) * scale, last_halo))

    args = [voltages, weights, voltages]
    specs = [
        pl.BlockSpec((n_block, STRETCH * FFT_LEN), lambda t: (ig, half * steps + t)),
        pl.BlockSpec((TAPS, 8, FFT_LEN), lambda t: (0, 0, 0)),
        pl.BlockSpec((n_block, TAPS * FFT_LEN), halo_at),
    ]
    if with_after:
        args.append(after)
        specs.append(pl.BlockSpec((n_block, after.shape[1]), lambda t: (ig, 0)))
    rows = n_in * SPAN
    out_shape = (FOLD // COLS, n_in, SPAN, COLS)
    folded = pl.pallas_call(
        functools.partial(filter_kernel, start % n_block, n_in, with_after),
        grid=(steps,),
        in_specs=specs + [pl.BlockSpec(memory_space=pl.ANY)] * len(deps),
        out_specs=[pl.BlockSpec((FOLD // COLS, n_in, STRETCH, COLS), lambda t: (0, 0, t, 0))] * 4,
        out_shape=[jax.ShapeDtypeStruct(out_shape, jnp.bfloat16)] * 4,
        scratch_shapes=[
            pltpu.VMEM((n_in * odd_stride(STRETCH), 128), jnp.float32),
            pltpu.VMEM((n_in * odd_stride(STRETCH), 128), jnp.float32),
            pltpu.VMEM((n_block, (TAPS - 1) * FFT_LEN), jnp.bfloat16),
        ],
        compiler_params=pltpu.CompilerParams(vmem_limit_bytes=VMEM),
        cost_estimate=pl.CostEstimate(
            flops=rows * FFT_LEN * TAPS * 2, bytes_accessed=rows * FFT_LEN * 6, transcendentals=0
        ),
        name="filter",
    )(*args, *deps)
    return [f.reshape(FOLD // COLS, rows, COLS) for f in folded]


def dft_kernel(*refs):
    folded, table_ref, (out_ref, held_ref) = refs[:4], refs[4], refs[-2:]
    step = pl.program_id(1)
    n_in = out_ref.shape[-2]
    n_rows = table_ref.shape[2] // 2
    pitch = odd_stride(n_in)
    n_chunks, f_rows, _ = folded[0].shape
    n_here = f_rows // SPAN

    def product(p, low_too, chunk, ref, rows):
        left = table_ref[0, p, : (1 + low_too) * n_rows, chunk * COLS : (chunk + 1) * COLS]
        dims = (((1,), (1,)), ((), ()))
        return lax.dot_general(left, ref[chunk, rows, :], dims, preferred_element_type=jnp.float32)

    for p in range(2):
        for pair in range(0, n_here, 2):
            take = min(2, n_here - pair)
            rows = pl.ds(pair * SPAN, take * SPAN)
            both = sum(product(p, 1, chunk, folded[2 * p], rows) for chunk in range(n_chunks))
            rest = sum(product(p, 0, chunk, folded[2 * p + 1], rows) for chunk in range(n_chunks))
            total = both[:n_rows] + (both[n_rows:] + rest)
            for j in range(take):
                at = step * n_here + pair + j
                held_ref[p, pl.ds(at, n_rows, stride=pitch), :] = total[:, j * SPAN : (j + 1) * SPAN]

    @pl.when(step == pl.num_programs(1) - 1)
    def _():
        n_dev, _, _, n_pair, _, _, _ = out_ref.shape
        for p in range(2):
            for d in range(n_dev):
                each = n_pair * 2 * pitch
                block = held_ref[p, pl.ds(d * each, each), :].reshape(n_pair, 2, pitch, SPAN)
                out_ref[d, 0, p] = block[:, :, :n_in].astype(jnp.bfloat16)


def dft_unit(folded, table, n_dev, n_in, g0, n_groups, n_slots, slot, previous, deps):
    chan_dev = CHANNELS // n_dev
    n_pair = chan_dev // GROUPS // 2
    n_rows = CHANNELS // GROUPS
    here = min(4, n_in)
    filled = [] if previous is None else [previous]
    f_block = (FOLD // COLS, here * SPAN, COLS)
    return pl.pallas_call(
        dft_kernel,
        grid=(n_groups, n_in // here),
        in_specs=[pl.BlockSpec(f_block, lambda g, i: (0, i, 0))] * 4
        + [pl.BlockSpec((1, 2, 2 * n_rows, FOLD), lambda g, i: (g0 + g, 0, 0, 0))]
        + [pl.BlockSpec(memory_space=pl.ANY)] * (len(deps) + len(filled)),
        out_specs=pl.BlockSpec(
            (n_dev, 1, 2, n_pair, 2, n_in, SPAN), lambda g, i: (0, slot + g, 0, 0, 0, 0, 0)
        ),
        out_shape=jax.ShapeDtypeStruct(
            (n_dev, n_slots, 2, n_pair, 2, n_in, SPAN), jnp.bfloat16
        ),
        input_output_aliases={5: 0} if filled else {},
        scratch_shapes=[pltpu.VMEM((2, n_rows * odd_stride(n_in), SPAN), jnp.float32)],
        compiler_params=pltpu.CompilerParams(vmem_limit_bytes=VMEM),
        cost_estimate=pl.CostEstimate(
            flops=n_groups * 12 * n_rows * n_in * SPAN * FOLD,
            bytes_accessed=n_groups * n_in * SPAN * FOLD * 8,
            transcendentals=0,
        ),
        name="dft",
    )(*folded, table, *filled, *deps)


def gram_kernel(layout, halves, n_wide, n_narrow, time_len, first, *refs):
    units = refs[: len(layout)]
    out_ref, both_ref, slot_ref, sems = refs[-4:]
    step, steps = pl.program_id(0), pl.num_programs(0)
    local_inputs = out_ref.shape[2] // n_wide

    def send(at, p, part):
        slot = lax.rem(at, 2)
        return pltpu.make_async_copy(
            slot_ref.at[slot, p, part], out_ref.at[first + 2 * at + p, part], sems.at[slot, p, part]
        )

    def wait_all(at):
        for p in range(2):
            for part in range(2):
                send(at, p, part).wait()

    @pl.when(step >= 2)
    def _():
        wait_all(step - 2)

    for p in range(2):
        for w in range(n_wide):
            for n in range(n_narrow):
                for unit, (start, n_in, half) in zip(units, layout):
                    row = pl.ds(w * local_inputs + start, n_in)
                    at = (n * halves + half) * SPAN
                    for part in range(2):
                        both_ref[p, row, pl.ds(part * time_len + at, SPAN)] = unit[
                            w * n_narrow + n, 0, p, 0, part
                        ]

    def product(left, right):
        dims = (((1,), (1,)), ((), ()))
        return lax.dot_general(left, right, dims, preferred_element_type=jnp.float32)

    scale = 1.0 / time_len
    for p in range(2):
        both, real, imag = both_ref[p], both_ref[p, :, :time_len], both_ref[p, :, time_len:]
        slot_ref[lax.rem(step, 2), p, 0] = product(both, both) * scale
        send(step, p, 0).start()
        cross = product(imag, real) * scale
        slot_ref[lax.rem(step, 2), p, 1] = cross - cross.T
        send(step, p, 1).start()

    @pl.when(step == steps - 1)
    def _():
        @pl.when(step >= 1)
        def _():
            wait_all(step - 1)

        wait_all(step)


def gram_group(units, layout, places, previous, n_wide, n_narrow, halves, inputs, group):
    n_dev = n_wide * n_narrow
    chan_dev = CHANNELS // n_dev
    cg = chan_dev // GROUPS
    n_units = len(units)
    time_len = n_narrow * halves * SPAN
    specs = [
        pl.BlockSpec(
            (n_dev, 1, 2, 1, 2, n_in, SPAN), lambda t, at=at: (0, at, 0, t, 0, 0, 0)
        )
        for at, (_, n_in, _) in zip(places, layout)
    ]
    args = list(units)
    aliases = {}
    if previous is not None:
        specs.append(pl.BlockSpec(memory_space=pl.ANY))
        args.append(previous)
        aliases = {n_units: 0}
    return pl.pallas_call(
        functools.partial(gram_kernel, layout, halves, n_wide, n_narrow, time_len, group * cg),
        grid=(cg // 2,),
        in_specs=specs,
        out_specs=pl.BlockSpec(memory_space=pl.ANY),
        out_shape=jax.ShapeDtypeStruct((chan_dev, 2, inputs, inputs), jnp.float32),
        scratch_shapes=[
            pltpu.VMEM((2, inputs, 2 * time_len), jnp.bfloat16),
            pltpu.VMEM((2, 2, 2, inputs, inputs), jnp.float32),
            pltpu.SemaphoreType.DMA((2, 2, 2)),
        ],
        input_output_aliases=aliases,
        compiler_params=pltpu.CompilerParams(vmem_limit_bytes=VMEM),
        cost_estimate=pl.CostEstimate(
            flops=cg * 8 * inputs * inputs * time_len,
            bytes_accessed=cg * inputs * (8 * inputs + 4 * time_len),
            transcendentals=0,
        ),
        name="gram",
    )(*args)


def shards(voltages, following):
    n_wide, n_narrow = lax.axis_size("wide"), lax.axis_size("narrow")
    n_dev = n_wide * n_narrow
    local_inputs, local_span = voltages.shape
    halves = local_span // (SPAN * FFT_LEN)

    leading = voltages[:, : (TAPS - 1) * FFT_LEN]
    shifted = lax.ppermute(leading, "narrow", [(i, i - 1) for i in range(1, n_narrow)])
    is_final = lax.axis_index("narrow") == n_narrow - 1
    after = jnp.where(is_final, following, shifted)

    table = jnp.asarray(dft_table(n_dev))
    weights = np.broadcast_to(pfb_window()[:, None, :], (TAPS, 8, FFT_LEN))
    weights = jnp.asarray(np.ascontiguousarray(weights))

    n_unit = min(16, local_inputs)
    layout = [
        (start, n_unit, half)
        for half in range(halves)
        for start in range(0, local_inputs, n_unit)
    ]
    if n_unit == 16:
        layout[:1] = [(0, 8, 0), (8, 8, 0)]
    last = len(layout) - 1
    parts = [[(0, 0, 1)], [(0, 1, GROUPS - 1)]]
    parts += [[(index, 0, GROUPS)] for index in range(1, last - 1)]
    parts += [[(last - 1, 0, GROUPS)]] if last > 1 else []
    parts[-1:] = [parts[-1] + [(last, 0, GROUPS - 1)]] if last > 1 else [parts[-1], [(last, 0, GROUPS - 1)]]
    parts += [[(last, GROUPS - 1, 1)]]

    received = []
    folded = {}
    place = {}
    for job, pieces in enumerate(parts):
        deps = [received[job - 2]] if job >= 2 else []
        n_slots = sum(size for _, _, size in pieces)
        spectra, slot = None, 0
        for index, first, size in pieces:
            start, n_in, half = layout[index]
            if index not in folded:
                folded[index] = filter_unit(
                    voltages, after, weights, start, n_in, half, halves, deps
                )
            spectra = dft_unit(
                folded[index], table, n_dev, n_in, first, size, n_slots, slot, spectra, deps
            )
            for group in range(first, first + size):
                place[index, group] = (job, slot + group - first)
            slot += size
        received.append(lax.all_to_all(spectra, AXES, split_axis=0, concat_axis=0, tiled=True))

    result = None
    for group in range(GROUPS):
        found = [place[index, group] for index in range(len(layout))]
        units = [received[job] for job, _ in found]
        places = [slot for _, slot in found]
        result = gram_group(
            units, layout, places, result, n_wide, n_narrow, halves, n_wide * local_inputs, group
        )
    return result


def solution(mesh):
    in_specs = (P("wide", "narrow"), P("wide", None))
    out_specs = P(("wide", "narrow"), None, None, None)
    return jax.shard_map(shards, mesh=mesh, in_specs=in_specs, out_specs=out_specs, check_vma=False)
```

```python
import functools
import itertools
import math

import jax
import jax.numpy as jnp
import ml_dtypes
import numpy as np
from jax import lax
from jax.experimental import pallas as pl
from jax.experimental.pallas import tpu as pltpu
from jax.sharding import PartitionSpec as P

FFT_LEN = 2048
CHANNELS = 1024
TAPS = 16
FOLD = FFT_LEN // 2
SPAN = 128
BATCH = 8
STRETCH = 32
COLS = 256
VMEM = 127 * 512 * 1024
AXES = ("wide", "narrow")


def group_count(n_dev):
    return min(8, CHANNELS // n_dev // 2)


def odd_stride(rows):
    return rows + 8 * (1 - rows // 8 % 2)


def pfb_window():
    n = np.arange(TAPS * FFT_LEN, dtype=np.float64)
    total = TAPS * FFT_LEN
    taper = 0.5 - 0.5 * np.cos(2.0 * np.pi * (n + 0.5) / total)
    window = np.sinc((n + 0.5 - total / 2) / FFT_LEN) * taper
    return window.astype(np.float32).reshape(TAPS, FFT_LEN)


def split16(values):
    high = values.astype(ml_dtypes.bfloat16)
    low = (values - high.astype(np.float64)).astype(ml_dtypes.bfloat16)
    return high, low


def dft_table(n_dev):
    chan_dev = CHANNELS // n_dev
    n_groups = group_count(n_dev)
    cg = chan_dev // n_groups
    g, p, d, h = np.meshgrid(
        np.arange(n_groups), np.arange(2), np.arange(n_dev), np.arange(cg // 2), indexing="ij"
    )
    chan = d * chan_dev + g * cg + 2 * h + p
    turns = chan[..., None] * np.arange(FOLD) % FFT_LEN
    angles = 2.0 * np.pi * turns / FFT_LEN
    table = np.stack([np.cos(angles), -np.sin(angles)], axis=-2) / math.sqrt(FFT_LEN)
    table = table.reshape(n_groups // 2, 2, 2, CHANNELS // n_groups, FOLD).swapaxes(1, 2)
    return np.stack(split16(table), axis=2)


def filter_kernel(first, n_in, with_after, x_ref, w_ref, halo_ref, *rest):
    outs, (even_ref, odd_ref, tail_ref) = rest[-7:-3], rest[-3:]
    n_rows = x_ref.shape[0]
    pitch = odd_stride(STRETCH)
    halo_len = (TAPS - 1) * FFT_LEN
    if with_after:
        is_last = pl.program_id(0) == pl.num_programs(0) - 1

        @pl.when(is_last)
        def _():
            tail_ref[...] = rest[0][:, :halo_len]

        @pl.when(jnp.logical_not(is_last))
        def _():
            tail_ref[...] = halo_ref[:, :halo_len]

        next_ref = tail_ref
    else:
        next_ref = halo_ref

    def load(t, k):
        ref, at = (x_ref, t) if t < STRETCH else (next_ref, t - STRETCH)
        tile = ref[:, pl.ds(pl.multiple_of(at * FFT_LEN + k, 128), 128)].astype(jnp.float32)
        return tile.reshape(n_rows // 8, 8, 128)[first // 8 : (first + n_in) // 8]

    def fir(m0, k):
        weights = [w_ref[p, :, pl.ds(pl.multiple_of(k, 128), 128)][None] for p in range(TAPS)]
        sums = [None] * BATCH
        for t in range(BATCH + TAPS - 1):
            tile = load(m0 + t, k)
            for j in range(max(0, t - TAPS + 1), min(BATCH, t + 1)):
                term = weights[t - j] * tile
                sums[j] = term if sums[j] is None else sums[j] + term
        return sums

    def columns(kt, _):
        k = kt * 128
        for m0 in range(0, STRETCH, BATCH):
            lower, upper = fir(m0, k), fir(m0, k + FOLD)
            for j in range(BATCH):
                rows = pl.ds(m0 + j, n_in, stride=pitch)
                even_ref[rows, :] = (lower[j] + upper[j]).reshape(n_in, 128)
                odd_ref[rows, :] = (lower[j] - upper[j]).reshape(n_in, 128)
        chunk, at = kt // (COLS // 128), pl.ds(pl.multiple_of(kt % (COLS // 128) * 128, 128), 128)
        for i in range(n_in):
            for p, ref in ((0, even_ref), (1, odd_ref)):
                value = ref[pl.ds(i * pitch, STRETCH), :]
                high = value.astype(jnp.bfloat16)
                low = (value - high.astype(jnp.float32)).astype(jnp.bfloat16)
                outs[2 * p][chunk, i, :, at] = high
                outs[2 * p + 1][chunk, i, :, at] = low
        return 0

    lax.fori_loop(0, FOLD // 128, columns, 0)


def filter_unit(voltages, after, weights, start, n_in, half, halves, deps):
    n_block = min(16, voltages.shape[0])
    ig = start // n_block
    steps = SPAN // STRETCH
    scale = STRETCH // TAPS
    last_halo = voltages.shape[1] // (TAPS * FFT_LEN) - 1
    with_after = half == halves - 1

    def halo_at(t):
        return (ig, jnp.minimum((half * steps + t + 1) * scale, last_halo))

    args = [voltages, weights, voltages]
    specs = [
        pl.BlockSpec((n_block, STRETCH * FFT_LEN), lambda t: (ig, half * steps + t)),
        pl.BlockSpec((TAPS, 8, FFT_LEN), lambda t: (0, 0, 0)),
        pl.BlockSpec((n_block, TAPS * FFT_LEN), halo_at),
    ]
    if with_after:
        args.append(after)
        specs.append(pl.BlockSpec((n_block, after.shape[1]), lambda t: (ig, 0)))
    rows = n_in * SPAN
    out_shape = (FOLD // COLS, n_in, SPAN, COLS)
    folded = pl.pallas_call(
        functools.partial(filter_kernel, start % n_block, n_in, with_after),
        grid=(steps,),
        in_specs=specs + [pl.BlockSpec(memory_space=pl.ANY)] * len(deps),
        out_specs=[pl.BlockSpec((FOLD // COLS, n_in, STRETCH, COLS), lambda t: (0, 0, t, 0))] * 4,
        out_shape=[jax.ShapeDtypeStruct(out_shape, jnp.bfloat16)] * 4,
        scratch_shapes=[
            pltpu.VMEM((n_in * odd_stride(STRETCH), 128), jnp.float32),
            pltpu.VMEM((n_in * odd_stride(STRETCH), 128), jnp.float32),
            pltpu.VMEM((n_block, (TAPS - 1) * FFT_LEN), jnp.bfloat16),
        ],
        compiler_params=pltpu.CompilerParams(vmem_limit_bytes=VMEM),
        cost_estimate=pl.CostEstimate(
            flops=rows * FFT_LEN * TAPS * 2, bytes_accessed=rows * FFT_LEN * 6, transcendentals=0
        ),
        name="filter",
    )(*args, *deps)
    return [f.reshape(FOLD // COLS, rows, COLS) for f in folded]


def dft_kernel(*refs):
    folded, table_ref, (out_ref, held_ref) = refs[:4], refs[4], refs[-2:]
    step = pl.program_id(1)
    n_in = out_ref.shape[-2]
    n_groups, n_rows = table_ref.shape[3], table_ref.shape[3] * table_ref.shape[4]
    pitch = odd_stride(n_in)
    n_chunks, f_rows, _ = folded[0].shape
    n_here = f_rows // SPAN

    def product(p, low_too, chunk, ref, rows):
        left = table_ref[0, p, : 1 + low_too, :, :, chunk * COLS : (chunk + 1) * COLS]
        left = left.reshape(-1, COLS)
        dims = (((1,), (1,)), ((), ()))
        return lax.dot_general(left, ref[chunk, rows, :], dims, preferred_element_type=jnp.float32)

    for p in range(2):
        high, low = folded[2 * p], folded[2 * p + 1]
        for pair in range(0, n_here, 2):
            take = min(2, n_here - pair)
            rows = pl.ds(pair * SPAN, take * SPAN)
            both = sum(product(p, 1, chunk, high, rows) for chunk in range(n_chunks))
            rest = sum(product(p, 0, chunk, low, rows) for chunk in range(n_chunks))
            total = both[:n_rows] + (both[n_rows:] + rest)
            for j in range(take):
                at = pl.ds(step * n_here + pair + j, n_rows, stride=pitch)
                held_ref[p, at, :] = total[:, j * SPAN : (j + 1) * SPAN]

    @pl.when(step == pl.num_programs(1) - 1)
    def _():
        n_dev, _, _, n_pair, _, _, _ = out_ref.shape
        each = n_pair * 2 * pitch
        for g, p, d in itertools.product(range(n_groups), range(2), range(n_dev)):
            block = held_ref[p, pl.ds((g * n_dev + d) * each, each), :].reshape(n_pair, 2, pitch, SPAN)
            out_ref[d, g, p] = block[:, :, :n_in].astype(jnp.bfloat16)


def dft_unit(folded, table, n_dev, n_in, g0, n_groups, n_slots, slot, previous, deps):
    chan_dev = CHANNELS // n_dev
    n_pair = chan_dev // group_count(n_dev) // 2
    n_rows = CHANNELS // group_count(n_dev)
    each = 1 if (g0 | n_groups | slot) % 2 else 2
    here = min(4, n_in)
    filled = [] if previous is None else [previous]

    def table_at(g, i):
        group = g0 + each * g
        return (group // 2, 0, 0, group % 2 if each == 1 else 0, 0, 0)

    f_block = (FOLD // COLS, here * SPAN, COLS)
    return pl.pallas_call(
        dft_kernel,
        grid=(n_groups // each, n_in // here),
        in_specs=[pl.BlockSpec(f_block, lambda g, i: (0, i, 0))] * 4
        + [pl.BlockSpec((1, 2, 2, each, n_rows, FOLD), table_at)]
        + [pl.BlockSpec(memory_space=pl.ANY)] * (len(deps) + len(filled)),
        out_specs=pl.BlockSpec(
            (n_dev, each, 2, n_pair, 2, n_in, SPAN),
            lambda g, i: (0, slot // each + g, 0, 0, 0, 0, 0),
        ),
        out_shape=jax.ShapeDtypeStruct(
            (n_dev, n_slots, 2, n_pair, 2, n_in, SPAN), jnp.bfloat16
        ),
        input_output_aliases={5: 0} if filled else {},
        scratch_shapes=[pltpu.VMEM((2, each * n_rows * odd_stride(n_in), SPAN), jnp.float32)],
        compiler_params=pltpu.CompilerParams(vmem_limit_bytes=VMEM),
        cost_estimate=pl.CostEstimate(
            flops=n_groups * 12 * n_rows * n_in * SPAN * FOLD,
            bytes_accessed=n_groups * n_in * SPAN * FOLD * 8,
            transcendentals=0,
        ),
        name="dft",
    )(*folded, table, *filled, *deps)


def gram_kernel(layout, halves, n_wide, n_narrow, time_len, first, *refs):
    units = refs[: len(layout)]
    out_ref, both_ref, slot_ref, sems = refs[-4:]
    step, steps = pl.program_id(0), pl.num_programs(0)
    local_inputs = out_ref.shape[2] // n_wide

    def send(at, p, part):
        slot = lax.rem(at, 2)
        return pltpu.make_async_copy(
            slot_ref.at[slot, p, part], out_ref.at[first + 2 * at + p, part], sems.at[slot, p, part]
        )

    def wait_all(at):
        for p in range(2):
            for part in range(2):
                send(at, p, part).wait()

    @pl.when(step >= 2)
    def _():
        wait_all(step - 2)

    for p in range(2):
        for w in range(n_wide):
            for n in range(n_narrow):
                for unit, (start, n_in, half) in zip(units, layout):
                    row = pl.ds(w * local_inputs + start, n_in)
                    at = (n * halves + half) * SPAN
                    for part in range(2):
                        both_ref[p, row, pl.ds(part * time_len + at, SPAN)] = unit[
                            w * n_narrow + n, 0, p, 0, part
                        ]

    def product(left, right):
        dims = (((1,), (1,)), ((), ()))
        return lax.dot_general(left, right, dims, preferred_element_type=jnp.float32)

    scale = 1.0 / time_len
    for p in range(2):
        both, real, imag = both_ref[p], both_ref[p, :, :time_len], both_ref[p, :, time_len:]
        slot_ref[lax.rem(step, 2), p, 0] = product(both, both) * scale
        send(step, p, 0).start()
        cross = product(imag, real) * scale
        slot_ref[lax.rem(step, 2), p, 1] = cross - cross.T
        send(step, p, 1).start()

    @pl.when(step == steps - 1)
    def _():
        @pl.when(step >= 1)
        def _():
            wait_all(step - 1)

        wait_all(step)


def gram_group(units, layout, places, previous, n_wide, n_narrow, halves, inputs, group):
    n_dev = n_wide * n_narrow
    chan_dev = CHANNELS // n_dev
    cg = chan_dev // group_count(n_dev)
    n_units = len(units)
    time_len = n_narrow * halves * SPAN
    specs = [
        pl.BlockSpec(
            (n_dev, 1, 2, 1, 2, n_in, SPAN), lambda t, at=at: (0, at, 0, t, 0, 0, 0)
        )
        for at, (_, n_in, _) in zip(places, layout)
    ]
    args = list(units)
    aliases = {}
    if previous is not None:
        specs.append(pl.BlockSpec(memory_space=pl.ANY))
        args.append(previous)
        aliases = {n_units: 0}
    return pl.pallas_call(
        functools.partial(gram_kernel, layout, halves, n_wide, n_narrow, time_len, group * cg),
        grid=(cg // 2,),
        in_specs=specs,
        out_specs=pl.BlockSpec(memory_space=pl.ANY),
        out_shape=jax.ShapeDtypeStruct((chan_dev, 2, inputs, inputs), jnp.float32),
        scratch_shapes=[
            pltpu.VMEM((2, inputs, 2 * time_len), jnp.bfloat16),
            pltpu.VMEM((2, 2, 2, inputs, inputs), jnp.float32),
            pltpu.SemaphoreType.DMA((2, 2, 2)),
        ],
        input_output_aliases=aliases,
        compiler_params=pltpu.CompilerParams(vmem_limit_bytes=VMEM),
        cost_estimate=pl.CostEstimate(
            flops=cg * 8 * inputs * inputs * time_len,
            bytes_accessed=cg * inputs * (8 * inputs + 4 * time_len),
            transcendentals=0,
        ),
        name="gram",
    )(*args)


def shards(voltages, following):
    n_wide, n_narrow = lax.axis_size("wide"), lax.axis_size("narrow")
    n_dev = n_wide * n_narrow
    local_inputs, local_span = voltages.shape
    halves = local_span // (SPAN * FFT_LEN)

    leading = voltages[:, : (TAPS - 1) * FFT_LEN]
    shifted = lax.ppermute(leading, "narrow", [(i, i - 1) for i in range(1, n_narrow)])
    is_final = lax.axis_index("narrow") == n_narrow - 1
    after = jnp.where(is_final, following, shifted)

    table = jnp.asarray(dft_table(n_dev))
    weights = np.broadcast_to(pfb_window()[:, None, :], (TAPS, 8, FFT_LEN))
    weights = jnp.asarray(np.ascontiguousarray(weights))

    n_unit = min(16, local_inputs)
    layout = [
        (start, n_unit, half)
        for half in range(halves)
        for start in range(0, local_inputs, n_unit)
    ]
    if n_unit == 16:
        layout[:1] = [(0, 8, 0), (8, 8, 0)]
    n_groups = group_count(n_dev)
    head, last = n_groups // 4, len(layout) - 1
    parts = [[(0, 0, head)], [(0, head, n_groups - head)]]
    if last > 1:
        parts += [[(index, 0, n_groups)] for index in range(1, last - 1)]
        parts += [[(last - 1, 0, n_groups - 2), (last - 1, n_groups - 2, 1)]]
        parts[-1] += [(last, n_groups - 2, 1), (last, 0, n_groups - 2)]
        parts += [[(last - 1, n_groups - 1, 1), (last, n_groups - 1, 1)]]
    else:
        parts += [[(last, 0, n_groups - 1)], [(last, n_groups - 1, 1)]]

    received = []
    folded = {}
    place = {}
    for job, pieces in enumerate(parts):
        deps = [received[job - 2]] if job >= 2 else []
        n_slots = sum(size for _, _, size in pieces)
        spectra, slot = None, 0
        for index, first, size in pieces:
            start, n_in, half = layout[index]
            if index not in folded:
                folded[index] = filter_unit(
                    voltages, after, weights, start, n_in, half, halves, deps
                )
            spectra = dft_unit(
                folded[index], table, n_dev, n_in, first, size, n_slots, slot, spectra, deps
            )
            for group in range(first, first + size):
                place[index, group] = (job, slot + group - first)
            slot += size
        received.append(lax.all_to_all(spectra, AXES, split_axis=0, concat_axis=0, tiled=True))

    result = None
    for group in range(n_groups):
        found = [place[index, group] for index in range(len(layout))]
        units = [received[job] for job, _ in found]
        places = [slot for _, slot in found]
        result = gram_group(
            units, layout, places, result, n_wide, n_narrow, halves, n_wide * local_inputs, group
        )
    return result


def solution(mesh):
    in_specs = (P("wide", "narrow"), P("wide", None))
    out_specs = P(("wide", "narrow"), None, None, None)
    return jax.shard_map(shards, mesh=mesh, in_specs=in_specs, out_specs=out_specs, check_vma=False)
```

```python
import functools
import itertools
import math

import jax
import jax.numpy as jnp
import ml_dtypes
import numpy as np
from jax import lax
from jax.experimental import pallas as pl
from jax.experimental.pallas import tpu as pltpu
from jax.sharding import PartitionSpec as P

FFT_LEN = 2048
CHANNELS = 1024
TAPS = 16
FOLD = FFT_LEN // 2
SPAN = 128
BATCH = 8
STRETCH = 32
COLS = 256
VMEM = 127 * 512 * 1024
AXES = ("wide", "narrow")


def group_count(n_dev):
    return min(8, CHANNELS // n_dev // 2)


def odd_stride(rows):
    return rows + 8 * (1 - rows // 8 % 2)


def pfb_window():
    n = np.arange(TAPS * FFT_LEN, dtype=np.float64)
    total = TAPS * FFT_LEN
    taper = 0.5 - 0.5 * np.cos(2.0 * np.pi * (n + 0.5) / total)
    window = np.sinc((n + 0.5 - total / 2) / FFT_LEN) * taper
    return window.astype(np.float32).reshape(TAPS, FFT_LEN)


def split16(values):
    high = values.astype(ml_dtypes.bfloat16)
    low = (values - high.astype(np.float64)).astype(ml_dtypes.bfloat16)
    return high, low


def dft_table(n_dev):
    chan_dev = CHANNELS // n_dev
    n_groups = group_count(n_dev)
    cg = chan_dev // n_groups
    g, p, d, h = np.meshgrid(
        np.arange(n_groups), np.arange(2), np.arange(n_dev), np.arange(cg // 2), indexing="ij"
    )
    chan = d * chan_dev + g * cg + 2 * h + p
    turns = chan[..., None] * np.arange(FOLD) % FFT_LEN
    angles = 2.0 * np.pi * turns / FFT_LEN
    table = np.stack([np.cos(angles), -np.sin(angles)], axis=-2) / math.sqrt(FFT_LEN)
    table = table.reshape(n_groups // 2, 2, 2, CHANNELS // n_groups, FOLD).swapaxes(1, 2)
    return np.stack(split16(table), axis=2)


def filter_kernel(first, n_in, with_after, x_ref, w_ref, halo_ref, *rest):
    outs, (even_ref, odd_ref, tail_ref) = rest[-7:-3], rest[-3:]
    n_rows = x_ref.shape[0]
    pitch = odd_stride(STRETCH)
    halo_len = (TAPS - 1) * FFT_LEN
    if with_after:
        is_last = pl.program_id(0) == pl.num_programs(0) - 1

        @pl.when(is_last)
        def _():
            tail_ref[...] = rest[0][:, :halo_len]

        @pl.when(jnp.logical_not(is_last))
        def _():
            tail_ref[...] = halo_ref[:, :halo_len]

        next_ref = tail_ref
    else:
        next_ref = halo_ref

    def load(t, k):
        ref, at = (x_ref, t) if t < STRETCH else (next_ref, t - STRETCH)
        tile = ref[:, pl.ds(pl.multiple_of(at * FFT_LEN + k, 128), 128)].astype(jnp.float32)
        return tile.reshape(n_rows // 8, 8, 128)[first // 8 : (first + n_in) // 8]

    def fir(m0, k):
        weights = [w_ref[p, :, pl.ds(pl.multiple_of(k, 128), 128)][None] for p in range(TAPS)]
        sums = [None] * BATCH
        for t in range(BATCH + TAPS - 1):
            tile = load(m0 + t, k)
            for j in range(max(0, t - TAPS + 1), min(BATCH, t + 1)):
                term = weights[t - j] * tile
                sums[j] = term if sums[j] is None else sums[j] + term
        return sums

    def columns(kt, _):
        k = kt * 128
        for m0 in range(0, STRETCH, BATCH):
            lower, upper = fir(m0, k), fir(m0, k + FOLD)
            for j in range(BATCH):
                rows = pl.ds(m0 + j, n_in, stride=pitch)
                even_ref[rows, :] = (lower[j] + upper[j]).reshape(n_in, 128)
                odd_ref[rows, :] = (lower[j] - upper[j]).reshape(n_in, 128)
        chunk, at = kt // (COLS // 128), pl.ds(pl.multiple_of(kt % (COLS // 128) * 128, 128), 128)
        for i in range(n_in):
            for p, ref in ((0, even_ref), (1, odd_ref)):
                value = ref[pl.ds(i * pitch, STRETCH), :]
                high = value.astype(jnp.bfloat16)
                low = (value - high.astype(jnp.float32)).astype(jnp.bfloat16)
                outs[2 * p][chunk, i, :, at] = high
                outs[2 * p + 1][chunk, i, :, at] = low
        return 0

    lax.fori_loop(0, FOLD // 128, columns, 0)


def filter_unit(voltages, after, weights, start, n_in, half, halves, deps):
    n_block = min(16, voltages.shape[0])
    ig = start // n_block
    steps = SPAN // STRETCH
    scale = STRETCH // TAPS
    last_halo = voltages.shape[1] // (TAPS * FFT_LEN) - 1
    with_after = half == halves - 1

    def halo_at(t):
        return (ig, jnp.minimum((half * steps + t + 1) * scale, last_halo))

    args = [voltages, weights, voltages]
    specs = [
        pl.BlockSpec((n_block, STRETCH * FFT_LEN), lambda t: (ig, half * steps + t)),
        pl.BlockSpec((TAPS, 8, FFT_LEN), lambda t: (0, 0, 0)),
        pl.BlockSpec((n_block, TAPS * FFT_LEN), halo_at),
    ]
    if with_after:
        args.append(after)
        specs.append(pl.BlockSpec((n_block, after.shape[1]), lambda t: (ig, 0)))
    rows = n_in * SPAN
    out_shape = (FOLD // COLS, n_in, SPAN, COLS)
    folded = pl.pallas_call(
        functools.partial(filter_kernel, start % n_block, n_in, with_after),
        grid=(steps,),
        in_specs=specs + [pl.BlockSpec(memory_space=pl.ANY)] * len(deps),
        out_specs=[pl.BlockSpec((FOLD // COLS, n_in, STRETCH, COLS), lambda t: (0, 0, t, 0))] * 4,
        out_shape=[jax.ShapeDtypeStruct(out_shape, jnp.bfloat16)] * 4,
        scratch_shapes=[
            pltpu.VMEM((n_in * odd_stride(STRETCH), 128), jnp.float32),
            pltpu.VMEM((n_in * odd_stride(STRETCH), 128), jnp.float32),
            pltpu.VMEM((n_block, (TAPS - 1) * FFT_LEN), jnp.bfloat16),
        ],
        compiler_params=pltpu.CompilerParams(vmem_limit_bytes=VMEM),
        cost_estimate=pl.CostEstimate(
            flops=rows * FFT_LEN * TAPS * 2, bytes_accessed=rows * FFT_LEN * 6, transcendentals=0
        ),
        name="filter",
    )(*args, *deps)
    return [f.reshape(FOLD // COLS, rows, COLS) for f in folded]


def dft_kernel(*refs):
    folded, table_ref, (out_ref, held_ref) = refs[:4], refs[4], refs[-2:]
    step = pl.program_id(1)
    n_in = out_ref.shape[-2]
    n_groups, n_rows = table_ref.shape[3], table_ref.shape[3] * table_ref.shape[4]
    pitch = odd_stride(n_in)
    n_chunks, f_rows, _ = folded[0].shape
    n_here = f_rows // SPAN

    def product(p, low_too, chunk, ref, rows):
        left = table_ref[0, p, : 1 + low_too, :, :, chunk * COLS : (chunk + 1) * COLS]
        left = left.reshape(-1, COLS)
        dims = (((1,), (1,)), ((), ()))
        return lax.dot_general(left, ref[chunk, rows, :], dims, preferred_element_type=jnp.float32)

    for p in range(2):
        high, low = folded[2 * p], folded[2 * p + 1]
        for pair in range(0, n_here, 2):
            take = min(2, n_here - pair)
            rows = pl.ds(pair * SPAN, take * SPAN)
            both = sum(product(p, 1, chunk, high, rows) for chunk in range(n_chunks))
            rest = sum(product(p, 0, chunk, low, rows) for chunk in range(n_chunks))
            total = both[:n_rows] + (both[n_rows:] + rest)
            for j in range(take):
                at = pl.ds(step * n_here + pair + j, n_rows, stride=pitch)
                held_ref[p, at, :] = total[:, j * SPAN : (j + 1) * SPAN]

    @pl.when(step == pl.num_programs(1) - 1)
    def _():
        n_dev, _, _, n_pair, _, _, _ = out_ref.shape
        each = n_pair * 2 * pitch
        for g, p, d in itertools.product(range(n_groups), range(2), range(n_dev)):
            block = held_ref[p, pl.ds((g * n_dev + d) * each, each), :].reshape(n_pair, 2, pitch, SPAN)
            out_ref[d, g, p] = block[:, :, :n_in].astype(jnp.bfloat16)


def dft_unit(folded, table, n_dev, n_in, g0, n_groups, n_slots, slot, previous, deps):
    chan_dev = CHANNELS // n_dev
    n_pair = chan_dev // group_count(n_dev) // 2
    n_rows = CHANNELS // group_count(n_dev)
    each = 1 if (g0 | n_groups | slot) % 2 else 2
    here = min(4, n_in)
    filled = [] if previous is None else [previous]

    def table_at(g, i):
        group = g0 + each * g
        return (group // 2, 0, 0, group % 2 if each == 1 else 0, 0, 0)

    f_block = (FOLD // COLS, here * SPAN, COLS)
    return pl.pallas_call(
        dft_kernel,
        grid=(n_groups // each, n_in // here),
        in_specs=[pl.BlockSpec(f_block, lambda g, i: (0, i, 0))] * 4
        + [pl.BlockSpec((1, 2, 2, each, n_rows, FOLD), table_at)]
        + [pl.BlockSpec(memory_space=pl.ANY)] * (len(deps) + len(filled)),
        out_specs=pl.BlockSpec(
            (n_dev, each, 2, n_pair, 2, n_in, SPAN),
            lambda g, i: (0, slot // each + g, 0, 0, 0, 0, 0),
        ),
        out_shape=jax.ShapeDtypeStruct(
            (n_dev, n_slots, 2, n_pair, 2, n_in, SPAN), jnp.bfloat16
        ),
        input_output_aliases={5: 0} if filled else {},
        scratch_shapes=[pltpu.VMEM((2, each * n_rows * odd_stride(n_in), SPAN), jnp.float32)],
        compiler_params=pltpu.CompilerParams(vmem_limit_bytes=VMEM),
        cost_estimate=pl.CostEstimate(
            flops=n_groups * 12 * n_rows * n_in * SPAN * FOLD,
            bytes_accessed=n_groups * n_in * SPAN * FOLD * 8,
            transcendentals=0,
        ),
        name="dft",
    )(*folded, table, *filled, *deps)


def gram_kernel(layout, halves, n_wide, n_narrow, time_len, first, *refs):
    units = refs[: len(layout)]
    out_ref, both_ref, slot_ref, sems = refs[-4:]
    step, steps = pl.program_id(0), pl.num_programs(0)
    local_inputs = out_ref.shape[2] // n_wide

    def send(at, p, part):
        slot = lax.rem(at, 2)
        return pltpu.make_async_copy(
            slot_ref.at[slot, p, part], out_ref.at[first + 2 * at + p, part], sems.at[slot, p, part]
        )

    def wait_all(at):
        for p in range(2):
            for part in range(2):
                send(at, p, part).wait()

    @pl.when(step >= 2)
    def _():
        wait_all(step - 2)

    for p in range(2):
        for w in range(n_wide):
            for n in range(n_narrow):
                for unit, (start, n_in, half) in zip(units, layout):
                    row = pl.ds(w * local_inputs + start, n_in)
                    at = (n * halves + half) * SPAN
                    for part in range(2):
                        both_ref[p, row, pl.ds(part * time_len + at, SPAN)] = unit[
                            w * n_narrow + n, 0, p, 0, part
                        ]

    def product(left, right):
        dims = (((1,), (1,)), ((), ()))
        return lax.dot_general(left, right, dims, preferred_element_type=jnp.float32)

    scale = 1.0 / time_len
    for p in range(2):
        both, real, imag = both_ref[p], both_ref[p, :, :time_len], both_ref[p, :, time_len:]
        slot_ref[lax.rem(step, 2), p, 0] = product(both, both) * scale
        send(step, p, 0).start()
        cross = product(imag, real) * scale
        slot_ref[lax.rem(step, 2), p, 1] = cross - cross.T
        send(step, p, 1).start()

    @pl.when(step == steps - 1)
    def _():
        @pl.when(step >= 1)
        def _():
            wait_all(step - 1)

        wait_all(step)


def gram_group(units, layout, places, previous, n_wide, n_narrow, halves, inputs, group, count):
    n_dev = n_wide * n_narrow
    chan_dev = CHANNELS // n_dev
    cg = chan_dev // group_count(n_dev)
    n_units = len(units)
    time_len = n_narrow * halves * SPAN
    specs = [
        pl.BlockSpec(
            (n_dev, 1, 2, 1, 2, n_in, SPAN), lambda t, at=at: (0, at + t // (cg // 2), 0, t % (cg // 2), 0, 0, 0)
        )
        for at, (_, n_in, _) in zip(places, layout)
    ]
    args = list(units)
    aliases = {}
    if previous is not None:
        specs.append(pl.BlockSpec(memory_space=pl.ANY))
        args.append(previous)
        aliases = {n_units: 0}
    return pl.pallas_call(
        functools.partial(gram_kernel, layout, halves, n_wide, n_narrow, time_len, group * cg),
        grid=(count * (cg // 2),),
        in_specs=specs,
        out_specs=pl.BlockSpec(memory_space=pl.ANY),
        out_shape=jax.ShapeDtypeStruct((chan_dev, 2, inputs, inputs), jnp.float32),
        scratch_shapes=[
            pltpu.VMEM((2, inputs, 2 * time_len), jnp.bfloat16),
            pltpu.VMEM((2, 2, 2, inputs, inputs), jnp.float32),
            pltpu.SemaphoreType.DMA((2, 2, 2)),
        ],
        input_output_aliases=aliases,
        compiler_params=pltpu.CompilerParams(vmem_limit_bytes=VMEM),
        cost_estimate=pl.CostEstimate(
            flops=count * cg * 8 * inputs * inputs * time_len,
            bytes_accessed=count * cg * inputs * (8 * inputs + 4 * time_len),
            transcendentals=0,
        ),
        name="gram",
    )(*args)


def shards(voltages, following):
    n_wide, n_narrow = lax.axis_size("wide"), lax.axis_size("narrow")
    n_dev = n_wide * n_narrow
    local_inputs, local_span = voltages.shape
    halves = local_span // (SPAN * FFT_LEN)

    leading = voltages[:, : (TAPS - 1) * FFT_LEN]
    shifted = lax.ppermute(leading, "narrow", [(i, i - 1) for i in range(1, n_narrow)])
    is_final = lax.axis_index("narrow") == n_narrow - 1
    after = jnp.where(is_final, following, shifted)

    table = jnp.asarray(dft_table(n_dev))
    weights = np.broadcast_to(pfb_window()[:, None, :], (TAPS, 8, FFT_LEN))
    weights = jnp.asarray(np.ascontiguousarray(weights))

    n_unit = min(16, local_inputs)
    layout = [
        (start, n_unit, half)
        for half in range(halves)
        for start in range(0, local_inputs, n_unit)
    ]
    if n_unit == 16:
        layout[:1] = [(0, 8, 0), (8, 8, 0)]
    n_groups = group_count(n_dev)
    head, last = max(n_groups // 8, 1), len(layout) - 1
    even = head + head % 2
    parts = [[(0, 0, head)], [(0, even, n_groups - even), (0, head, even - head)]]
    if last > 1:
        parts += [[(index, 0, n_groups)] for index in range(1, last - 1)]
        parts += [[(last - 1, 0, n_groups - 2), (last - 1, n_groups - 2, 1)]]
        parts[-1] += [(last, n_groups - 2, 1), (last, 0, n_groups - 2)]
        parts += [[(last - 1, n_groups - 1, 1), (last, n_groups - 1, 1)]]
    else:
        parts += [[(last, 0, n_groups - 1)], [(last, n_groups - 1, 1)]]

    received = []
    folded = {}
    place = {}
    for job, pieces in enumerate(parts):
        deps = [received[job - 2]] if job >= 2 else []
        n_slots = sum(size for _, _, size in pieces)
        spectra, slot = None, 0
        for index, first, size in pieces:
            start, n_in, half = layout[index]
            if index not in folded:
                folded[index] = filter_unit(
                    voltages, after, weights, start, n_in, half, halves, deps
                )
            spectra = dft_unit(
                folded[index], table, n_dev, n_in, first, size, n_slots, slot, spectra, deps
            )
            for group in range(first, first + size):
                place[index, group] = (job, slot + group - first)
            slot += size
        received.append(lax.all_to_all(spectra, AXES, split_axis=0, concat_axis=0, tiled=True))

    result = None
    runs = []
    for group in range(n_groups):
        found = [place[index, group] for index in range(len(layout))]
        if runs and found == [(job, slot + runs[-1][1]) for job, slot in runs[-1][2]]:
            runs[-1][1] += 1
        else:
            runs.append([group, 1, found])
    for group, count, found in runs:
        units = [received[job] for job, _ in found]
        places = [slot for _, slot in found]
        result = gram_group(
            units,
            layout,
            places,
            result,
            n_wide,
            n_narrow,
            halves,
            n_wide * local_inputs,
            group,
            count,
        )
    return result


def solution(mesh):
    in_specs = (P("wide", "narrow"), P("wide", None))
    out_specs = P(("wide", "narrow"), None, None, None)
    return jax.shard_map(shards, mesh=mesh, in_specs=in_specs, out_specs=out_specs, check_vma=False)
```
